32 devices in a mesh: groups: 2 (over y), tiles: 8 (over z, x), section: 2 (over core).
Axes of the slice: x: 2, y: 2, z: 4, core: 2. Of those that a mesh axis runs over, the one named last changes fastest.
Arguments:
- object_slices: float32 [2, 2, 1024, 1024], P(None, 'section', ('groups', 'tiles')), parts along dimension 2
- probe_wave: float32 [2, 128, 128], replicated, may hold values from -4 to 4
- propagator: float32 [2, 128, 128], replicated
- tile_counts: int32 [16], P(('groups', 'tiles')), parts along dimension 0, may hold values from 0 to 12, as said below
- row_offsets: int32 [192], P(('groups', 'tiles')), parts along dimension 0, may hold values from 0 to 63
- column_offsets: int32 [192], P(('groups', 'tiles')), parts along dimension 0, may hold values from 0 to 896
- intensity: float32 [192, 128, 128], P(('groups', 'tiles')), parts along dimension 0, may hold values from 0 to 2
Outputs:
- object_grad: float32 [2, 2, 1024, 1024], P(None, 'section', ('groups', 'tiles')), parts along dimension 2
The draws below stay inside these ranges and needn't reach their ends.
There are 2 independent parts, one for each index of `groups`. The reference program is written for one: setup_inputs(seed, part) draws one part's arguments, and reference() takes and returns one part's arrays. A program takes and returns all parts, laid end to end along the dimension named above; an argument that names none is the same for every part. Nothing has to cross between parts.
Inputs may be any that keep to these rules, and one draw needn't show every extreme that they name: Tile i owns the positions in its first tile_counts[i] slots; the last two tiles own none; all counts sum to 32; the positions of tiles 0 to i - 1 number at least 4 * i, and those of tiles 0 to i at most 4 * (i + 3).
All inputs are finite; a program needn't handle non-finite values.
Results may differ from the reference program's by a relative error of at most 0.014.
The reference program's roundings to bfloat16 on the way count: a program that leaves them out, or rounds other values in their place, can miss the bound.
Values may be sent and summed in bfloat16 or wider, within the bound.
A program may use at most 64 MiB of HBM per device.

```python
import math
import jax
import jax.numpy as jnp
from jax import lax

W = 128
TH = 64
OW = 1024
BAL = 4
CAP = 12
SLICES = 2
OH = 512
N_TILES = 8


def draw_object_slices(key, part):
    first_key, second_key = jax.random.split(jax.random.fold_in(key, 11))
    shape = (SLICES, OH, OW)
    amplitude = jax.random.uniform(first_key, shape, jnp.float32, 0.6, 1.0)
    phases = jax.random.uniform(second_key, shape, jnp.float32, -math.pi, math.pi)
    return jnp.stack([amplitude * jnp.cos(phases), amplitude * jnp.sin(phases)])


def draw_propagator(key, part):
    odd_scale = 2 * jax.random.randint(jax.random.fold_in(key, 13), (), 0, 32) + 1
    counter = jnp.arange(W, dtype=jnp.int32)
    offsets = (counter[:, None] - counter[None, :] + W // 2) % W - W // 2
    turned = odd_scale * offsets * offsets % (2 * W)
    angles = turned.astype(jnp.float32) * (math.pi / W)
    factor = 1.0 / math.sqrt(W)
    return jnp.stack([jnp.cos(angles) * factor, jnp.sin(angles) * factor])


def draw_tile_counts(key, part):
    first_key, second_key = jax.random.split(jax.random.fold_in(key, 17))
    worker = jnp.arange(N_TILES, dtype=jnp.int32)[:, None]
    lowest = jnp.maximum(0, worker - (N_TILES - 3))
    highest = jnp.minimum(2, worker)
    step_back = jax.random.randint(first_key, (N_TILES, BAL), lowest, highest + 1)
    busiest = jax.random.randint(second_key, (), 0, N_TILES - 2)
    forced = worker - busiest
    step_back = jnp.where((forced >= 0) & (forced <= 2), forced, step_back)
    owners = worker - step_back
    tile_ids = jnp.arange(N_TILES, dtype=jnp.int32)
    return jnp.sum((owners[:, :, None] == tile_ids[None, None, :]).astype(jnp.int32), axis=(0, 1))


def draw_row_offsets(key, part):
    first_key, second_key = jax.random.split(jax.random.fold_in(key, 19))
    values = jax.random.randint(first_key, (N_TILES * CAP,), 0, TH)
    chosen = jax.random.randint(second_key, (2,), 0, N_TILES * CAP)
    counter = jnp.arange(N_TILES * CAP, dtype=jnp.int32)
    values = jnp.where(counter == chosen[0], TH - 1, values)
    return jnp.where(counter == chosen[1], 0, values)


def draw_column_offsets(key, part):
    first_key, second_key = jax.random.split(jax.random.fold_in(key, 23))
    values = jax.random.randint(first_key, (N_TILES * CAP,), 0, OW - W + 1)
    chosen = jax.random.randint(second_key, (2,), 0, N_TILES * CAP)
    counter = jnp.arange(N_TILES * CAP, dtype=jnp.int32)
    values = jnp.where(counter == chosen[0], OW - W, values)
    return jnp.where(counter == chosen[1], 0, values)


def shard_levels(stream_key, dims, cuts, low, top_value):
    def one(position, shards_of):
        draws = jax.random.uniform(jax.random.fold_in(jax.random.fold_in(stream_key, 6), position), (shards_of,), jnp.float32, low / len(cuts), top_value / len(cuts))
        return jnp.repeat(jnp.exp(draws), dims[position] // shards_of).reshape((-1,) + (1,) * (len(dims) - position - 1))

    gain = one(*cuts[0])
    for cut in cuts[1:]:
        gain = gain * one(*cut)
    return gain


def scatter_about(key, extent, scale, most, held_as=jnp.bfloat16):
    return jnp.clip(scale * jax.random.normal(key, extent, jnp.float32), -most, most).astype(held_as)


def setup_inputs(seed: int = 0, part: int = 0) -> dict:
    keys = jax.random.split(jax.random.key(seed), 8)
    part_keys = jax.random.split(jax.random.fold_in(keys[7], part), 8)
    object_slices = draw_object_slices(jax.random.fold_in(jax.random.fold_in(keys[7], part), 71), part)
    probe_wave = scatter_about(keys[1], (2, W, W), 0.7, 4.0, jnp.float32)
    propagator = draw_propagator(jax.random.fold_in(keys[7], 71), part)
    tile_counts = draw_tile_counts(jax.random.fold_in(jax.random.fold_in(keys[7], part), 71), part)
    row_offsets = draw_row_offsets(jax.random.fold_in(jax.random.fold_in(keys[7], part), 71), part)
    column_offsets = draw_column_offsets(jax.random.fold_in(jax.random.fold_in(keys[7], part), 71), part)
    intensity = jnp.clip(2.0 * jax.random.uniform(part_keys[6], (N_TILES * CAP, W, W), jnp.float32) ** shard_levels(part_keys[6], (N_TILES * CAP, W, W), ((0, 8),), -0.2, 0.2), 0.0, 2.0)
    return {"object_slices": object_slices, "probe_wave": probe_wave, "propagator": propagator, "tile_counts": tile_counts, "row_offsets": row_offsets, "column_offsets": column_offsets, "intensity": intensity}


def fourier_table(wave_size):
    counter = jnp.arange(wave_size, dtype=jnp.int32)
    turned = counter[:, None] * counter[None, :] % wave_size
    angles = turned.astype(jnp.float32) * (2.0 * math.pi / wave_size)
    factor = 1.0 / math.sqrt(wave_size)
    return jnp.stack([jnp.cos(angles) * factor, -jnp.sin(angles) * factor])

def conjugate(matrix):
    return jnp.stack([matrix[0], -matrix[1]])

def widened(values):
    return lax.optimization_barrier(values).astype(jnp.float32)

def complex_left(matrix, wavefield):
    products = jnp.einsum('cmn,bdnk->bcdmk', widened(matrix), widened(wavefield), precision=lax.Precision.HIGHEST)
    return jnp.stack([products[:, 0, 0] - products[:, 1, 1], products[:, 0, 1] + products[:, 1, 0]], axis=1)

def complex_right(wavefield, matrix):
    products = jnp.einsum('bdmn,cnk->bdcmk', widened(wavefield), widened(matrix), precision=lax.Precision.HIGHEST)
    return jnp.stack([products[:, 0, 0] - products[:, 1, 1], products[:, 0, 1] + products[:, 1, 0]], axis=1)

def sandwich(matrix, wavefield):
    halfway = complex_left(matrix, wavefield).astype(jnp.bfloat16)
    return complex_right(halfway, matrix)

def complex_times(left_side, right_side):
    return jnp.stack([left_side[:, 0] * right_side[:, 0] - left_side[:, 1] * right_side[:, 1], left_side[:, 0] * right_side[:, 1] + left_side[:, 1] * right_side[:, 0]], axis=1)

def conjugate_times(left_side, right_side):
    return jnp.stack([left_side[:, 0] * right_side[:, 0] + left_side[:, 1] * right_side[:, 1], left_side[:, 0] * right_side[:, 1] - left_side[:, 1] * right_side[:, 0]], axis=1)

def forward_slices(wavefield, patches, propagator_b):
    saved_waves = []
    for layer_index in range(patches.shape[2]):
        saved_waves.append(wavefield)
        product = complex_times(widened(wavefield), patches[:, :, layer_index]).astype(jnp.bfloat16)
        wavefield = sandwich(propagator_b, product).astype(jnp.bfloat16)
    return (wavefield, jnp.stack(saved_waves, axis=2))

def far_field(wavefield, measured, live_slots, fourier_b):
    far_wave = sandwich(fourier_b, wavefield)
    excess = far_wave[:, 0] * far_wave[:, 0] + far_wave[:, 1] * far_wave[:, 1] - measured
    misfit = (far_wave * (excess * live_slots[:, None, None])[:, None]).astype(jnp.bfloat16)
    return sandwich(conjugate(fourier_b), misfit).astype(jnp.bfloat16)

def backward_slices(adjoint, patches, saved_waves, propagator_conj):
    gradients = [None] * patches.shape[2]
    for layer_index in reversed(range(patches.shape[2])):
        backward = sandwich(propagator_conj, adjoint)
        gradients[layer_index] = conjugate_times(widened(saved_waves[:, :, layer_index]), backward)
        adjoint = conjugate_times(patches[:, :, layer_index], backward).astype(jnp.bfloat16)
    return (adjoint, jnp.stack(gradients, axis=2))

def reference(object_slices, probe_wave, propagator, tile_counts, row_offsets, column_offsets, intensity):
    wave_size = probe_wave.shape[1]
    slice_count = object_slices.shape[1]
    fourier_b = fourier_table(wave_size).astype(jnp.bfloat16)
    propagator_b = propagator.astype(jnp.bfloat16)
    propagator_conj = conjugate(propagator_b)
    start_wave = probe_wave.astype(jnp.bfloat16)[None]
    zero_index = jnp.zeros((), jnp.int32)

    def visit(counter, summed):
        counter = jnp.asarray(counter).astype(jnp.int32)
        owner_tile = counter // CAP
        slot_number = counter % CAP

        def work(summed):
            top_row = (owner_tile * TH + row_offsets[counter]).astype(jnp.int32)
            left_edge = column_offsets[counter].astype(jnp.int32)
            corner = (zero_index, zero_index, top_row, left_edge)
            patches = lax.dynamic_slice(object_slices, corner, (2, slice_count, wave_size, wave_size))[None]
            exit_wave, saved_waves = forward_slices(start_wave, patches, propagator_b)
            adjoint = far_field(exit_wave, intensity[counter][None], jnp.ones((1,), jnp.float32), fourier_b)
            adjoint, gradients = backward_slices(adjoint, patches, saved_waves, propagator_conj)
            current = lax.dynamic_slice(summed, corner, gradients.shape[1:])
            return lax.dynamic_update_slice(summed, current + gradients[0], corner)
        return lax.cond(slot_number < tile_counts[owner_tile], work, lambda unchanged: unchanged, summed)
    return lax.fori_loop(0, N_TILES * CAP, visit, jnp.zeros(object_slices.shape, jnp.float32))
```

```python
import math

import jax
import jax.numpy as jnp
import numpy as np
from jax import lax
from jax.experimental import pallas as pl
from jax.experimental.pallas import tpu as pltpu
from jax.sharding import PartitionSpec as P

MESH = pl.DeviceIdType.MESH
BF16 = jnp.bfloat16
F32 = jnp.float32


def fourier_blocks(wave_size):
    counter = np.arange(wave_size)
    turned = (counter[:, None] * counter[None, :] % wave_size).astype(np.float32)
    angles = turned * np.float32(2.0 * math.pi / wave_size)
    factor = np.float32(1.0 / math.sqrt(wave_size))
    real = (np.cos(angles) * factor).astype(np.float32)
    imag = (-np.sin(angles) * factor).astype(np.float32)
    plain = np.block([[real, imag], [-imag, real]])
    turned = np.block([[real, -imag], [imag, real]])
    return jnp.asarray(np.stack([plain, turned]).astype(jnp.bfloat16))


def dot(left_side, right_side):
    return jnp.dot(left_side, right_side, preferred_element_type=F32)


def sandwich(left_block, right_block, waves):
    size = waves[0][0].shape[0]
    stacked = jnp.concatenate([jnp.concatenate([real, imag], axis=0) for real, imag in waves], axis=1)
    halfway = dot(left_block, stacked).astype(BF16)
    results = []
    for p in range(len(waves)):
        columns = slice(p * size, (p + 1) * size)
        row = jnp.concatenate([halfway[:size, columns], halfway[size:, columns]], axis=1)
        full = dot(row, right_block)
        results.append((full[:, :size], full[:, size:]))
    return results


def times(a, b):
    return (a[0] * b[0] - a[1] * b[1], a[0] * b[1] + a[1] * b[0])


def conj_times(a, b):
    return (a[0] * b[0] + a[1] * b[1], a[0] * b[1] - a[1] * b[0])


def cast(pair, dtype):
    return (pair[0].astype(dtype), pair[1].astype(dtype))


def kernel(
    tile_count, counts, row_offsets, column_offsets, object_ref, probe_ref, propagator_ref,
    fourier_ref, intensity_hbm, out_ref, bands, strips, pick, place, pick_rows, place_rows, partial, to_partner,
    from_partner, to_tiles, from_tiles, measured, send_sem, recv_sem, load_sem,
):
    size = probe_ref.shape[1]
    rows = object_ref.shape[2]
    width = object_ref.shape[3]
    mine = measured.shape[0]
    tile = lax.axis_index("tiles")
    core = lax.axis_index("section")
    other = 1 - core
    first = core * mine

    load = pltpu.make_async_copy(intensity_hbm.at[pl.ds(first, mine)], measured, load_sem)
    load.start()

    def remote(src, dst, index, where):
        return pltpu.make_async_remote_copy(
            src_ref=src, dst_ref=dst, send_sem=send_sem.at[index], recv_sem=recv_sem.at[index],
            device_id=where, device_id_type=MESH,
        )

    partner = {"section": other}

    def towards(step):
        return {"tiles": tile + step}

    barrier = pltpu.get_barrier_semaphore()
    pl.semaphore_signal(barrier, inc=1, device_id=partner, device_id_type=MESH)
    arrivals = jnp.int32(1)
    for step in (-2, -1, 1, 2):
        there = (tile + step >= 0) & (tile + step < tile_count)
        arrivals = arrivals + there.astype(jnp.int32)

        @pl.when(there)
        def _():
            pl.semaphore_signal(barrier, inc=1, device_id=towards(step), device_id_type=MESH)

    for plane in range(2):
        bands[core, 0, plane * rows : (plane + 1) * rows, :] = object_ref[plane, 0].astype(BF16)
    pl.semaphore_wait(barrier, arrivals)

    own = remote(bands.at[core, 0], bands.at[core, 0], 0, partner)
    for ahead in (1, 2):

        @pl.when(tile >= ahead)
        def _():
            remote(bands.at[core, 0], bands.at[core, ahead], ahead, towards(-ahead)).start()

    own.start()

    spots = lax.broadcasted_iota(jnp.int32, (size, width), 1)
    counter = lax.broadcasted_iota(jnp.int32, (size, width), 0)
    down_spots = lax.broadcasted_iota(jnp.int32, (width, size), 0)
    down_counter = lax.broadcasted_iota(jnp.int32, (width, size), 1)
    row_spots = lax.broadcasted_iota(jnp.int32, (size, 3 * rows), 1)
    row_counter = lax.broadcasted_iota(jnp.int32, (size, 3 * rows), 0)
    down_row_spots = lax.broadcasted_iota(jnp.int32, (3 * rows, size), 0)
    down_row_counter = lax.broadcasted_iota(jnp.int32, (3 * rows, size), 1)
    for p in range(mine):
        column = column_offsets[first + p]
        offset = row_offsets[first + p]
        pick[:, p * size : (p + 1) * size] = jnp.where(down_spots == down_counter + column, 1.0, 0.0).astype(BF16)
        place[p * size : (p + 1) * size, :] = jnp.where(spots == counter + column, 1.0, 0.0).astype(BF16)
        pick_rows[p] = jnp.where(row_spots == row_counter + offset, 1.0, 0.0).astype(BF16)
        place_rows[p] = jnp.where(down_row_spots == down_row_counter + offset, 1.0, 0.0).astype(BF16)
    prop = (propagator_ref[0].astype(BF16), propagator_ref[1].astype(BF16))

    def block(a, b, c, d):
        return jnp.concatenate([jnp.concatenate([a, b], axis=1), jnp.concatenate([c, d], axis=1)], axis=0)

    prop_plain = block(prop[0], prop[1], -prop[1], prop[0])
    prop_turned = block(prop[0], -prop[1], prop[1], prop[0])
    four_plain = fourier_ref[0]
    four_turned = fourier_ref[1]

    def extract(layer, b):
        found = dot(bands[layer, b], pick[...]).astype(BF16)
        for p in range(mine):
            for plane in range(2):
                strips[layer, p, b * rows : (b + 1) * rows, plane * size : (plane + 1) * size] = found[
                    plane * rows : (plane + 1) * rows, p * size : (p + 1) * size
                ]

    for ahead in (1, 2):

        @pl.when(tile + ahead >= tile_count)
        def _():
            for layer in range(2):
                bands[layer, ahead] = jnp.zeros((2 * rows, width), BF16)

    extract(core, 0)
    own.wait()
    extract(other, 0)
    for ahead in (1, 2):

        @pl.when(tile + ahead < tile_count)
        def _():
            here = bands.at[core, ahead]
            remote(here, here, ahead, partner).wait_recv()
            remote(here, here, 2 + ahead, partner).start()

        extract(core, ahead)

    for ahead in (1, 2):

        @pl.when(tile + ahead < tile_count)
        def _():
            here = bands.at[core, ahead]
            there = bands.at[other, ahead]
            remote(there, there, 2 + ahead, partner).wait_recv()
            remote(here, here, 2 + ahead, partner).wait_send()

        @pl.when(tile >= ahead)
        def _():
            remote(bands.at[core, 0], bands.at[core, ahead], ahead, towards(-ahead)).wait_send()

        extract(other, ahead)

    patches = [[None] * mine for _ in range(2)]
    for layer in range(2):
        for p in range(mine):
            found = dot(pick_rows[p], strips[layer, p])
            patches[layer][p] = (found[:, :size], found[:, size:])

    start = (probe_ref[0].astype(BF16).astype(F32), probe_ref[1].astype(BF16).astype(F32))
    product = [cast(times(start, patches[0][p]), BF16) for p in range(mine)]
    middle = [cast(z, BF16) for z in sandwich(prop_turned, prop_plain, product)]
    product = [cast(times(cast(middle[p], F32), patches[1][p]), BF16) for p in range(mine)]
    exit_waves = [cast(z, BF16) for z in sandwich(prop_turned, prop_plain, product)]
    far = sandwich(four_turned, four_plain, exit_waves)
    load.wait()
    misfit = []
    for p in range(mine):
        real, imag = far[p]
        excess = real * real + imag * imag - measured[p]
        live = jnp.full((size, size), first + p, jnp.int32) < counts[0]
        misfit.append(
            (jnp.where(live, excess * real, 0.0).astype(BF16), jnp.where(live, excess * imag, 0.0).astype(BF16))
        )
    adjoint = [cast(z, BF16) for z in sandwich(four_plain, four_turned, misfit)]

    def deposit(layer, gradients):
        shifted = [
            dot(place_rows[p], jnp.concatenate(cast(gradients[p], BF16), axis=1)).astype(BF16) for p in range(mine)
        ]
        for b in (1, 2, 0):
            pieces = [
                jnp.concatenate(
                    [s[b * rows : (b + 1) * rows, plane * size : (plane + 1) * size] for s in shifted], axis=1
                )
                for plane in range(2)
            ]
            partial[layer, b] = dot(jnp.concatenate(pieces, axis=0), place[...])

    back = sandwich(prop_plain, prop_turned, adjoint)
    deposit(1, [conj_times(cast(middle[p], F32), back[p]) for p in range(mine)])
    adjoint = [cast(conj_times(patches[1][p], back[p]), BF16) for p in range(mine)]
    back = sandwich(prop_plain, prop_turned, adjoint)
    deposit(0, [conj_times(start, back[p]) for p in range(mine)])

    swaps = []
    for b in (1, 2, 0):
        to_partner[b] = partial[other, b].astype(BF16)
        swap = remote(to_partner.at[b], from_partner.at[b], 5 + b, partner)
        swap.start()
        swaps.append(swap)
    for b, swap in zip((1, 2), swaps):
        swap.wait()
        to_tiles[b - 1] = (partial[core, b] + from_partner[b].astype(F32)).astype(BF16)

        @pl.when(tile + b < tile_count)
        def _():
            remote(to_tiles.at[b - 1], from_tiles.at[b - 1], 7 + b, towards(b)).start()

    swaps[2].wait()
    total = partial[core, 0] + from_partner[0].astype(F32)
    for plane in range(2):
        out_ref[plane, 0] = total[plane * rows : (plane + 1) * rows]
    for b in (1, 2):

        @pl.when(tile >= b)
        def _():
            remote(to_tiles.at[b - 1], from_tiles.at[b - 1], 7 + b, partner).wait_recv()
            for plane in range(2):
                out_ref[plane, 0] += from_tiles[b - 1, plane * rows : (plane + 1) * rows, :].astype(F32)

    for b in (1, 2):

        @pl.when(tile + b < tile_count)
        def _():
            remote(to_tiles.at[b - 1], from_tiles.at[b - 1], 7 + b, partner).wait_send()


def shards(
    object_slices, probe_wave, propagator, tile_counts, row_offsets, column_offsets, intensity
):
    size = probe_wave.shape[1]
    rows, width = object_slices.shape[2:]
    mine = row_offsets.shape[0] // lax.axis_size("section")
    tile_count = lax.axis_size("tiles")
    smem = pl.BlockSpec(memory_space=pltpu.SMEM)
    vmem = pl.BlockSpec(memory_space=pltpu.VMEM)

    def body(*refs):
        kernel(tile_count, *refs)

    return pl.pallas_call(
        body,
        out_shape=jax.ShapeDtypeStruct(object_slices.shape, F32),
        in_specs=[smem, smem, smem, vmem, vmem, vmem, vmem, pl.BlockSpec(memory_space=pl.ANY)],
        out_specs=vmem,
        scratch_shapes=[
            pltpu.VMEM((2, 3, 2 * rows, width), BF16),
            pltpu.VMEM((2, mine, 3 * rows, 2 * size), BF16),
            pltpu.VMEM((width, mine * size), BF16),
            pltpu.VMEM((mine * size, width), BF16),
            pltpu.VMEM((mine, size, 3 * rows), BF16),
            pltpu.VMEM((mine, 3 * rows, size), BF16),
            pltpu.VMEM((2, 3, 2 * rows, width), F32),
            pltpu.VMEM((3, 2 * rows, width), BF16),
            pltpu.VMEM((3, 2 * rows, width), BF16),
            pltpu.VMEM((2, 2 * rows, width), BF16),
            pltpu.VMEM((2, 2 * rows, width), BF16),
            pltpu.VMEM((mine, size, size), F32),
            pltpu.SemaphoreType.DMA((10,)),
            pltpu.SemaphoreType.DMA((10,)),
            pltpu.SemaphoreType.DMA,
        ],
        compiler_params=pltpu.CompilerParams(
            collective_id=0, has_side_effects=True, vmem_limit_bytes=48 * 1024 * 1024
        ),
    )(
        tile_counts, row_offsets, column_offsets, object_slices, probe_wave, propagator,
        fourier_blocks(size), intensity,
    )


def solution(mesh):
    placed = (
        P(None, "section", ("groups", "tiles"), None),
        P(),
        P(),
        P(("groups", "tiles")),
        P(("groups", "tiles")),
        P(("groups", "tiles")),
        P(("groups", "tiles"), None, None),
    )
    return jax.shard_map(
        shards,
        mesh=mesh,
        in_specs=placed,
        out_specs=P(None, "section", ("groups", "tiles"), None),
        check_vma=False,
    )
```

```python
import math

import jax
import jax.numpy as jnp
import numpy as np
from jax import lax
from jax.experimental import pallas as pl
from jax.experimental.pallas import tpu as pltpu
from jax.sharding import PartitionSpec as P

MESH = pl.DeviceIdType.MESH
BF16 = jnp.bfloat16
CHUNKS = 4
F32 = jnp.float32


def fourier_blocks(wave_size):
    counter = np.arange(wave_size)
    turned = (counter[:, None] * counter[None, :] % wave_size).astype(np.float32)
    angles = turned * np.float32(2.0 * math.pi / wave_size)
    factor = np.float32(1.0 / math.sqrt(wave_size))
    real = (np.cos(angles) * factor).astype(np.float32)
    imag = (-np.sin(angles) * factor).astype(np.float32)
    plain = np.block([[real, imag], [-imag, real]])
    turned = np.block([[real, -imag], [imag, real]])
    return jnp.asarray(np.stack([plain, turned]).astype(jnp.bfloat16))


def dot(left_side, right_side):
    return jnp.dot(left_side, right_side, preferred_element_type=F32)


def sandwich(left_block, right_block, waves):
    size = waves[0][0].shape[0]
    stacked = jnp.concatenate([jnp.concatenate([real, imag], axis=0) for real, imag in waves], axis=1)
    halfway = dot(left_block, stacked).astype(BF16)
    results = []
    for p in range(len(waves)):
        columns = slice(p * size, (p + 1) * size)
        row = jnp.concatenate([halfway[:size, columns], halfway[size:, columns]], axis=1)
        full = dot(row, right_block)
        results.append((full[:, :size], full[:, size:]))
    return results


def times(a, b):
    return (a[0] * b[0] - a[1] * b[1], a[0] * b[1] + a[1] * b[0])


def conj_times(a, b):
    return (a[0] * b[0] + a[1] * b[1], a[0] * b[1] - a[1] * b[0])


def cast(pair, dtype):
    return (pair[0].astype(dtype), pair[1].astype(dtype))


def kernel(
    tile_count, counts_hbm, row_offsets_hbm, column_offsets_hbm, object_hbm, probe_hbm, propagator_hbm,
    fourier_hbm, intensity_hbm, out_ref, counts, row_offsets, column_offsets, object_ref, probe_ref,
    propagator_ref, fourier_ref, measured, bands, strips, pick, place, pick_rows, place_rows, partial,
    to_partner, from_partner, to_next, to_mate, from_back, from_mate, relayed, send_sem, recv_sem, load_sem,
):
    size = probe_ref.shape[1]
    rows = object_ref.shape[2]
    width = object_ref.shape[3]
    mine = measured.shape[0]
    tile = lax.axis_index("tiles")
    core = lax.axis_index("section")
    other = 1 - core
    first = core * mine
    odd = lax.rem(tile, 2) == 1
    even = lax.rem(tile, 2) == 0
    mate = tile + 1 - 2 * lax.rem(tile, 2)
    has_mate = mate < tile_count

    loads = [
        pltpu.make_async_copy(source, held, load_sem.at[i])
        for i, (source, held) in enumerate(
            [
                (object_hbm, object_ref),
                (row_offsets_hbm, row_offsets),
                (column_offsets_hbm, column_offsets),
                (counts_hbm, counts),
                (propagator_hbm, propagator_ref),
                (fourier_hbm, fourier_ref),
                (probe_hbm, probe_ref),
                (intensity_hbm.at[pl.ds(first, mine)], measured),
            ]
        )
    ]
    for load in loads:
        load.start()

    def remote(src, dst, index, where):
        return pltpu.make_async_remote_copy(
            src_ref=src, dst_ref=dst, send_sem=send_sem.at[index], recv_sem=recv_sem.at[index],
            device_id=where, device_id_type=MESH,
        )

    partner = {"section": other}
    to_back = {"tiles": tile - 2}
    to_ahead = {"tiles": tile + 2}
    across = {"tiles": mate}

    barrier = pltpu.get_barrier_semaphore()
    pl.semaphore_signal(barrier, inc=1, device_id=partner, device_id_type=MESH)
    arrivals = jnp.int32(1)
    for there, where in ((tile >= 2, to_back), (tile + 2 < tile_count, to_ahead), (has_mate, across)):
        arrivals = arrivals + there.astype(jnp.int32)

        @pl.when(there)
        def _():
            pl.semaphore_signal(barrier, inc=1, device_id=where, device_id_type=MESH)

    loads[0].wait()
    for plane in range(2):
        bands[core, 0, plane * rows : (plane + 1) * rows, :] = object_ref[plane, 0].astype(BF16)
    pl.semaphore_wait(barrier, arrivals)

    piece = 2 * rows // CHUNKS

    def part(c):
        return pl.ds(c * piece, piece)

    def chunk(layer, b, c):
        return bands.at[layer, b, part(c)]

    def band_copy(layer, source, target, c, kind, where):
        return remote(chunk(layer, source, c), chunk(layer, target, c), CHUNKS * kind + c, where)

    @pl.when(tile >= 2)
    def _():
        for c in range(CHUNKS):
            band_copy(core, 0, 2, c, 2, to_back).start()

    @pl.when(odd)
    def _():
        for c in range(CHUNKS):
            band_copy(core, 0, 1, c, 1, across).start()

    for c in range(CHUNKS):
        band_copy(core, 0, 0, c, 0, partner).start()

    for load in loads[1:7]:
        load.wait()

    spots = lax.broadcasted_iota(jnp.int32, (size, width), 1)
    counter = lax.broadcasted_iota(jnp.int32, (size, width), 0)
    down_spots = lax.broadcasted_iota(jnp.int32, (width, size), 0)
    down_counter = lax.broadcasted_iota(jnp.int32, (width, size), 1)
    row_spots = lax.broadcasted_iota(jnp.int32, (size, 3 * rows), 1)
    row_counter = lax.broadcasted_iota(jnp.int32, (size, 3 * rows), 0)
    down_row_spots = lax.broadcasted_iota(jnp.int32, (3 * rows, size), 0)
    down_row_counter = lax.broadcasted_iota(jnp.int32, (3 * rows, size), 1)
    for p in range(mine):
        column = column_offsets[first + p]
        offset = row_offsets[first + p]
        pick[:, p * size : (p + 1) * size] = jnp.where(down_spots == down_counter + column, 1.0, 0.0).astype(BF16)
        place[p * size : (p + 1) * size, :] = jnp.where(spots == counter + column, 1.0, 0.0).astype(BF16)
        pick_rows[p] = jnp.where(row_spots == row_counter + offset, 1.0, 0.0).astype(BF16)
        place_rows[p] = jnp.where(down_row_spots == down_row_counter + offset, 1.0, 0.0).astype(BF16)
    prop = (propagator_ref[0].astype(BF16), propagator_ref[1].astype(BF16))

    def block(a, b, c, d):
        return jnp.concatenate([jnp.concatenate([a, b], axis=1), jnp.concatenate([c, d], axis=1)], axis=0)

    prop_plain = block(prop[0], prop[1], -prop[1], prop[0])
    prop_turned = block(prop[0], -prop[1], prop[1], prop[0])
    four_plain = fourier_ref[0]
    four_turned = fourier_ref[1]

    def extract(layer, b):
        found = dot(bands[layer, b], pick[...]).astype(BF16)
        for p in range(mine):
            for plane in range(2):
                strips[layer, p, b * rows : (b + 1) * rows, plane * size : (plane + 1) * size] = found[
                    plane * rows : (plane + 1) * rows, p * size : (p + 1) * size
                ]

    for ahead in (1, 2):

        @pl.when(tile + ahead >= tile_count)
        def _():
            for layer in range(2):
                bands[layer, ahead] = jnp.zeros((2 * rows, width), BF16)

    extract(core, 0)
    for c in range(CHUNKS):
        band_copy(core, 0, 0, c, 0, partner).wait()
    extract(other, 0)

    @pl.when(tile + 2 < tile_count)
    def _():
        for c in range(CHUNKS):
            band_copy(core, 2, 2, c, 2, partner).wait_recv()

            @pl.when(even)
            def _():
                band_copy(core, 2, 1, c, 1, across).start()

            band_copy(core, 2, 2, c, 4, partner).start()

    extract(core, 2)

    @pl.when(tile + 1 < tile_count)
    def _():
        for c in range(CHUNKS):
            band_copy(core, 1, 1, c, 1, partner).wait_recv()
            band_copy(core, 1, 1, c, 3, partner).start()

    extract(core, 1)

    @pl.when(tile + 2 < tile_count)
    def _():
        for c in range(CHUNKS):
            band_copy(other, 2, 2, c, 4, partner).wait_recv()

    extract(other, 2)

    @pl.when(tile + 1 < tile_count)
    def _():
        for c in range(CHUNKS):
            band_copy(other, 1, 1, c, 3, partner).wait_recv()

    extract(other, 1)

    patches = [[None] * mine for _ in range(2)]
    for layer in range(2):
        for p in range(mine):
            found = dot(pick_rows[p], strips[layer, p])
            patches[layer][p] = (found[:, :size], found[:, size:])

    start = (probe_ref[0].astype(BF16).astype(F32), probe_ref[1].astype(BF16).astype(F32))
    product = [cast(times(start, patches[0][p]), BF16) for p in range(mine)]
    middle = [cast(z, BF16) for z in sandwich(prop_turned, prop_plain, product)]
    product = [cast(times(cast(middle[p], F32), patches[1][p]), BF16) for p in range(mine)]
    exit_waves = [cast(z, BF16) for z in sandwich(prop_turned, prop_plain, product)]
    far = sandwich(four_turned, four_plain, exit_waves)
    loads[7].wait()
    misfit = []
    for p in range(mine):
        real, imag = far[p]
        excess = real * real + imag * imag - measured[p]
        live = jnp.full((size, size), first + p, jnp.int32) < counts[0]
        misfit.append(
            (jnp.where(live, excess * real, 0.0).astype(BF16), jnp.where(live, excess * imag, 0.0).astype(BF16))
        )
    adjoint = [cast(z, BF16) for z in sandwich(four_plain, four_turned, misfit)]

    def deposit(layer, gradients):
        shifted = [
            dot(place_rows[p], jnp.concatenate(cast(gradients[p], BF16), axis=1)).astype(BF16) for p in range(mine)
        ]
        for b in (1, 2, 0):
            pieces = [
                jnp.concatenate(
                    [s[b * rows : (b + 1) * rows, plane * size : (plane + 1) * size] for s in shifted], axis=1
                )
                for plane in range(2)
            ]
            partial[layer, b] = dot(jnp.concatenate(pieces, axis=0), place[...])

    def swap(b):
        return remote(to_partner.at[b], from_partner.at[b], 5 * CHUNKS + b, partner)

    def piece_copy(source, target, c, kind, where):
        return remote(source.at[part(c)], target.at[part(c)], CHUNKS * kind + c, where)

    def give(layer):
        @pl.when(core != layer)
        def _():
            for b in (1, 2, 0):
                to_partner[b] = partial[layer, b].astype(BF16)
                swap(b).start()

    def hand_over(layer):
        @pl.when(core == layer)
        def _():
            swap(1).wait_recv()
            for c in range(CHUNKS):
                to_mate[part(c)] = (partial[layer, 1, part(c)] + from_partner[1, part(c)].astype(F32)).astype(BF16)

                @pl.when(even & has_mate)
                def _():
                    piece_copy(to_mate, from_mate, c, 6, across).start()

                @pl.when(odd & (tile + 1 < tile_count))
                def _():
                    piece_copy(to_mate, relayed, c, 7, across).start()

            swap(2).wait_recv()

            @pl.when(tile + 2 < tile_count)
            def _():
                for c in range(CHUNKS):
                    total = partial[layer, 2, part(c)] + from_partner[2, part(c)].astype(F32)

                    @pl.when(odd)
                    def _():
                        to_next[part(c)] = total.astype(BF16)

                    @pl.when(even)
                    def _():
                        piece_copy(to_mate, relayed, c, 7, across).wait_recv()
                        to_next[part(c)] = (total + relayed[part(c)].astype(F32)).astype(BF16)

                    piece_copy(to_next, from_back, c, 8, to_ahead).start()

    back = sandwich(prop_plain, prop_turned, adjoint)
    deposit(1, [conj_times(cast(middle[p], F32), back[p]) for p in range(mine)])
    give(1)
    adjoint = [cast(conj_times(patches[1][p], back[p]), BF16) for p in range(mine)]
    back = sandwich(prop_plain, prop_turned, adjoint)
    gradients = [conj_times(start, back[p]) for p in range(mine)]
    hand_over(1)
    deposit(0, gradients)
    give(0)
    hand_over(0)

    swap(0).wait_recv()
    total = partial[core, 0] + from_partner[0].astype(F32)
    for plane in range(2):
        out_ref[plane, 0] = total[plane * rows : (plane + 1) * rows]

    def add_in(received, kind):
        for c in range(CHUNKS):
            piece_copy(received, received, c, kind, across).wait_recv()
            plane, inside = divmod(c * piece, rows)
            out_ref[plane, 0, inside : inside + piece] += received[part(c)].astype(F32)

    @pl.when(odd)
    def _():
        add_in(from_mate, 6)

    @pl.when(tile >= 2)
    def _():
        add_in(from_back, 8)

    @pl.when(tile >= 2)
    def _():
        for c in range(CHUNKS):
            band_copy(core, 0, 2, c, 2, partner).wait_send()

    @pl.when(odd)
    def _():
        for c in range(CHUNKS):
            band_copy(core, 0, 1, c, 1, partner).wait_send()

    @pl.when(tile + 2 < tile_count)
    def _():
        @pl.when(even)
        def _():
            for c in range(CHUNKS):
                band_copy(core, 2, 1, c, 1, partner).wait_send()

        for c in range(CHUNKS):
            band_copy(core, 2, 2, c, 4, partner).wait_send()
        for c in range(CHUNKS):
            piece_copy(to_next, from_back, c, 8, partner).wait_send()

    @pl.when(tile + 1 < tile_count)
    def _():
        for c in range(CHUNKS):
            band_copy(core, 1, 1, c, 3, partner).wait_send()

    for b in range(3):
        swap(b).wait_send()

    @pl.when(even & has_mate)
    def _():
        for c in range(CHUNKS):
            piece_copy(to_mate, from_mate, c, 6, partner).wait_send()

    @pl.when(odd & (tile + 1 < tile_count))
    def _():
        for c in range(CHUNKS):
            piece_copy(to_mate, relayed, c, 7, partner).wait_send()


def shards(
    object_slices, probe_wave, propagator, tile_counts, row_offsets, column_offsets, intensity
):
    size = probe_wave.shape[1]
    rows, width = object_slices.shape[2:]
    mine = row_offsets.shape[0] // lax.axis_size("section")
    tile_count = lax.axis_size("tiles")
    anywhere = pl.BlockSpec(memory_space=pl.ANY)
    vmem = pl.BlockSpec(memory_space=pltpu.VMEM)
    band = pltpu.VMEM((2 * rows, width), BF16)

    def body(*refs):
        kernel(tile_count, *refs)

    return pl.pallas_call(
        body,
        out_shape=jax.ShapeDtypeStruct(object_slices.shape, F32),
        in_specs=[anywhere] * 8,
        out_specs=vmem,
        scratch_shapes=[
            pltpu.SMEM(tile_counts.shape, jnp.int32),
            pltpu.SMEM(row_offsets.shape, jnp.int32),
            pltpu.SMEM(column_offsets.shape, jnp.int32),
            pltpu.VMEM(object_slices.shape, F32),
            pltpu.VMEM(probe_wave.shape, F32),
            pltpu.VMEM(propagator.shape, F32),
            pltpu.VMEM((2, 2 * size, 2 * size), BF16),
            pltpu.VMEM((mine, size, size), F32),
            pltpu.VMEM((2, 3, 2 * rows, width), BF16),
            pltpu.VMEM((2, mine, 3 * rows, 2 * size), BF16),
            pltpu.VMEM((width, mine * size), BF16),
            pltpu.VMEM((mine * size, width), BF16),
            pltpu.VMEM((mine, size, 3 * rows), BF16),
            pltpu.VMEM((mine, 3 * rows, size), BF16),
            pltpu.VMEM((2, 3, 2 * rows, width), F32),
            pltpu.VMEM((3, 2 * rows, width), BF16),
            pltpu.VMEM((3, 2 * rows, width), BF16),
            band,
            band,
            band,
            band,
            band,
            pltpu.SemaphoreType.DMA((9 * CHUNKS,)),
            pltpu.SemaphoreType.DMA((9 * CHUNKS,)),
            pltpu.SemaphoreType.DMA((8,)),
        ],
        compiler_params=pltpu.CompilerParams(
            collective_id=0, has_side_effects=True, vmem_limit_bytes=60 * 1024 * 1024
        ),
    )(
        tile_counts, row_offsets, column_offsets, object_slices, probe_wave, propagator,
        fourier_blocks(size), intensity,
    )


def solution(mesh):
    placed = (
        P(None, "section", ("groups", "tiles"), None),
        P(),
        P(),
        P(("groups", "tiles")),
        P(("groups", "tiles")),
        P(("groups", "tiles")),
        P(("groups", "tiles"), None, None),
    )
    return jax.shard_map(
        shards,
        mesh=mesh,
        in_specs=placed,
        out_specs=P(None, "section", ("groups", "tiles"), None),
        check_vma=False,
    )
```

```python
import math

import jax
import jax.numpy as jnp
import numpy as np
from jax import lax
from jax.experimental import pallas as pl
from jax.experimental.pallas import tpu as pltpu
from jax.sharding import PartitionSpec as P

MESH = pl.DeviceIdType.MESH
BF16 = jnp.bfloat16
CHUNKS = 8
F32 = jnp.float32


def fourier_blocks(wave_size):
    counter = np.arange(wave_size)
    turned = (counter[:, None] * counter[None, :] % wave_size).astype(np.float32)
    angles = turned * np.float32(2.0 * math.pi / wave_size)
    factor = np.float32(1.0 / math.sqrt(wave_size))
    real = (np.cos(angles) * factor).astype(np.float32)
    imag = (-np.sin(angles) * factor).astype(np.float32)
    plain = np.block([[real, imag], [-imag, real]])
    turned = np.block([[real, -imag], [imag, real]])
    return jnp.asarray(np.stack([plain, turned]).astype(jnp.bfloat16))


def dot(left_side, right_side):
    return jnp.dot(left_side, right_side, preferred_element_type=F32)


def sandwich(left_block, right_block, waves):
    size = waves[0][0].shape[0]
    stacked = jnp.concatenate([jnp.concatenate([real, imag], axis=0) for real, imag in waves], axis=1)
    halfway = dot(left_block, stacked).astype(BF16)
    results = []
    for p in range(len(waves)):
        columns = slice(p * size, (p + 1) * size)
        row = jnp.concatenate([halfway[:size, columns], halfway[size:, columns]], axis=1)
        full = dot(row, right_block)
        results.append((full[:, :size], full[:, size:]))
    return results


def times(a, b):
    return (a[0] * b[0] - a[1] * b[1], a[0] * b[1] + a[1] * b[0])


def conj_times(a, b):
    return (a[0] * b[0] + a[1] * b[1], a[0] * b[1] - a[1] * b[0])


def cast(pair, dtype):
    return (pair[0].astype(dtype), pair[1].astype(dtype))


def kernel(
    tile_count, counts_hbm, row_offsets_hbm, column_offsets_hbm, object_hbm, probe_hbm, propagator_hbm,
    fourier_hbm, intensity_hbm, out_ref, counts, row_offsets, column_offsets, object_ref, probe_ref,
    propagator_ref, fourier_ref, measured, bands, strips, pick, place, pick_rows, place_rows, partial,
    to_partner, from_partner, to_next, to_mate, from_back, from_mate, relayed, send_sem, recv_sem, load_sem,
):
    size = probe_ref.shape[1]
    rows = object_ref.shape[2]
    width = object_ref.shape[3]
    mine = measured.shape[0]
    tile = lax.axis_index("tiles")
    core = lax.axis_index("section")
    other = 1 - core
    first = core * mine
    odd = lax.rem(tile, 2) == 1
    even = lax.rem(tile, 2) == 0
    mate = tile + 1 - 2 * lax.rem(tile, 2)
    has_mate = mate < tile_count

    loads = [
        pltpu.make_async_copy(source, held, load_sem.at[i])
        for i, (source, held) in enumerate(
            [
                (object_hbm, object_ref),
                (row_offsets_hbm, row_offsets),
                (column_offsets_hbm, column_offsets),
                (counts_hbm, counts),
                (propagator_hbm, propagator_ref),
                (fourier_hbm, fourier_ref),
                (probe_hbm, probe_ref),
                (intensity_hbm.at[pl.ds(first, mine)], measured),
            ]
        )
    ]
    for load in loads:
        load.start()

    def remote(src, dst, index, where):
        return pltpu.make_async_remote_copy(
            src_ref=src, dst_ref=dst, send_sem=send_sem.at[index], recv_sem=recv_sem.at[index],
            device_id=where, device_id_type=MESH,
        )

    partner = {"section": other}
    to_back = {"tiles": tile - 2}
    to_ahead = {"tiles": tile + 2}
    across = {"tiles": mate}

    barrier = pltpu.get_barrier_semaphore()
    pl.semaphore_signal(barrier, inc=1, device_id=partner, device_id_type=MESH)
    arrivals = jnp.int32(1)
    for there, where in ((tile >= 2, to_back), (tile + 2 < tile_count, to_ahead), (has_mate, across)):
        arrivals = arrivals + there.astype(jnp.int32)

        @pl.when(there)
        def _():
            pl.semaphore_signal(barrier, inc=1, device_id=where, device_id_type=MESH)

    loads[0].wait()
    for plane in range(2):
        bands[core, 0, plane * rows : (plane + 1) * rows, :] = object_ref[plane, 0].astype(BF16)
    pl.semaphore_wait(barrier, arrivals)

    piece = 2 * rows // CHUNKS

    def part(c):
        return pl.ds(c * piece, piece)

    def chunk(layer, b, c):
        return bands.at[layer, b, part(c)]

    def band_copy(layer, source, target, c, kind, where):
        return remote(chunk(layer, source, c), chunk(layer, target, c), CHUNKS * kind + c, where)

    @pl.when(tile >= 2)
    def _():
        for c in range(CHUNKS):
            band_copy(core, 0, 2, c, 2, to_back).start()

    @pl.when(odd)
    def _():
        for c in range(CHUNKS):
            band_copy(core, 0, 1, c, 1, across).start()

    for c in range(CHUNKS):
        band_copy(core, 0, 0, c, 0, partner).start()

    for load in loads[1:7]:
        load.wait()

    spots = lax.broadcasted_iota(jnp.int32, (size, width), 1)
    counter = lax.broadcasted_iota(jnp.int32, (size, width), 0)
    down_spots = lax.broadcasted_iota(jnp.int32, (width, size), 0)
    down_counter = lax.broadcasted_iota(jnp.int32, (width, size), 1)
    row_spots = lax.broadcasted_iota(jnp.int32, (size, 3 * rows), 1)
    row_counter = lax.broadcasted_iota(jnp.int32, (size, 3 * rows), 0)
    down_row_spots = lax.broadcasted_iota(jnp.int32, (3 * rows, size), 0)
    down_row_counter = lax.broadcasted_iota(jnp.int32, (3 * rows, size), 1)
    for p in range(mine):
        column = column_offsets[first + p]
        offset = row_offsets[first + p]
        pick[:, p * size : (p + 1) * size] = jnp.where(down_spots == down_counter + column, 1.0, 0.0).astype(BF16)
        place[p * size : (p + 1) * size, :] = jnp.where(spots == counter + column, 1.0, 0.0).astype(BF16)
        pick_rows[p] = jnp.where(row_spots == row_counter + offset, 1.0, 0.0).astype(BF16)
        place_rows[p] = jnp.where(down_row_spots == down_row_counter + offset, 1.0, 0.0).astype(BF16)
    prop = (propagator_ref[0].astype(BF16), propagator_ref[1].astype(BF16))

    def block(a, b, c, d):
        return jnp.concatenate([jnp.concatenate([a, b], axis=1), jnp.concatenate([c, d], axis=1)], axis=0)

    prop_plain = block(prop[0], prop[1], -prop[1], prop[0])
    prop_turned = block(prop[0], -prop[1], prop[1], prop[0])
    four_plain = fourier_ref[0]
    four_turned = fourier_ref[1]

    def extract(layer, b):
        found = dot(bands[layer, b], pick[...]).astype(BF16)
        for p in range(mine):
            for plane in range(2):
                strips[layer, p, b * rows : (b + 1) * rows, plane * size : (plane + 1) * size] = found[
                    plane * rows : (plane + 1) * rows, p * size : (p + 1) * size
                ]

    for ahead in (1, 2):

        @pl.when(tile + ahead >= tile_count)
        def _():
            for layer in range(2):
                bands[layer, ahead] = jnp.zeros((2 * rows, width), BF16)

    extract(core, 0)
    for c in range(CHUNKS):
        band_copy(core, 0, 0, c, 0, partner).wait()
    extract(other, 0)

    @pl.when(tile + 2 < tile_count)
    def _():
        for c in range(CHUNKS):
            band_copy(core, 2, 2, c, 2, partner).wait_recv()

            @pl.when(even)
            def _():
                band_copy(core, 2, 1, c, 1, across).start()

            band_copy(core, 2, 2, c, 4, partner).start()

    extract(core, 2)

    @pl.when(tile + 1 < tile_count)
    def _():
        for c in range(CHUNKS):
            band_copy(core, 1, 1, c, 1, partner).wait_recv()
            band_copy(core, 1, 1, c, 3, partner).start()

    extract(core, 1)

    @pl.when(tile + 2 < tile_count)
    def _():
        for c in range(CHUNKS):
            band_copy(other, 2, 2, c, 4, partner).wait_recv()

    extract(other, 2)

    @pl.when(tile + 1 < tile_count)
    def _():
        for c in range(CHUNKS):
            band_copy(other, 1, 1, c, 3, partner).wait_recv()

    extract(other, 1)

    patches = [[None] * mine for _ in range(2)]
    for layer in range(2):
        for p in range(mine):
            found = dot(pick_rows[p], strips[layer, p])
            patches[layer][p] = (found[:, :size], found[:, size:])

    start = (probe_ref[0].astype(BF16).astype(F32), probe_ref[1].astype(BF16).astype(F32))
    product = [cast(times(start, patches[0][p]), BF16) for p in range(mine)]
    middle = [cast(z, BF16) for z in sandwich(prop_turned, prop_plain, product)]
    product = [cast(times(cast(middle[p], F32), patches[1][p]), BF16) for p in range(mine)]
    exit_waves = [cast(z, BF16) for z in sandwich(prop_turned, prop_plain, product)]
    far = sandwich(four_turned, four_plain, exit_waves)
    loads[7].wait()
    misfit = []
    for p in range(mine):
        real, imag = far[p]
        excess = real * real + imag * imag - measured[p]
        live = jnp.full((size, size), first + p, jnp.int32) < counts[0]
        misfit.append(
            (jnp.where(live, excess * real, 0.0).astype(BF16), jnp.where(live, excess * imag, 0.0).astype(BF16))
        )
    adjoint = [cast(z, BF16) for z in sandwich(four_plain, four_turned, misfit)]

    def deposit(layer, gradients):
        shifted = [
            dot(place_rows[p], jnp.concatenate(cast(gradients[p], BF16), axis=1)).astype(BF16) for p in range(mine)
        ]
        for b in (1, 2, 0):
            pieces = [
                jnp.concatenate(
                    [s[b * rows : (b + 1) * rows, plane * size : (plane + 1) * size] for s in shifted], axis=1
                )
                for plane in range(2)
            ]
            partial[layer, b] = dot(jnp.concatenate(pieces, axis=0), place[...])

    def swap(b):
        return remote(to_partner.at[b], from_partner.at[b], 5 * CHUNKS + b, partner)

    def piece_copy(source, target, c, kind, where):
        return remote(source.at[part(c)], target.at[part(c)], CHUNKS * kind + c, where)

    def give(layer):
        @pl.when(core != layer)
        def _():
            for b in (1, 2, 0):
                to_partner[b] = partial[layer, b].astype(BF16)
                swap(b).start()

    def hand_over(layer):
        @pl.when(core == layer)
        def _():
            swap(1).wait_recv()
            for c in range(CHUNKS):
                to_mate[part(c)] = (partial[layer, 1, part(c)] + from_partner[1, part(c)].astype(F32)).astype(BF16)

                @pl.when(even & has_mate)
                def _():
                    piece_copy(to_mate, from_mate, c, 6, across).start()

                @pl.when(odd & (tile + 1 < tile_count))
                def _():
                    piece_copy(to_mate, relayed, c, 7, across).start()

            swap(2).wait_recv()

            @pl.when(tile + 2 < tile_count)
            def _():
                for c in range(CHUNKS):
                    total = partial[layer, 2, part(c)] + from_partner[2, part(c)].astype(F32)

                    @pl.when(odd)
                    def _():
                        to_next[part(c)] = total.astype(BF16)

                    @pl.when(even)
                    def _():
                        piece_copy(to_mate, relayed, c, 7, across).wait_recv()
                        to_next[part(c)] = (total + relayed[part(c)].astype(F32)).astype(BF16)

                    piece_copy(to_next, from_back, c, 8, to_ahead).start()

    back = sandwich(prop_plain, prop_turned, adjoint)
    deposit(1, [conj_times(cast(middle[p], F32), back[p]) for p in range(mine)])
    give(1)
    adjoint = [cast(conj_times(patches[1][p], back[p]), BF16) for p in range(mine)]
    back = sandwich(prop_plain, prop_turned, adjoint)
    gradients = [conj_times(start, back[p]) for p in range(mine)]
    hand_over(1)
    deposit(0, gradients)
    give(0)
    hand_over(0)

    swap(0).wait_recv()
    total = partial[core, 0] + from_partner[0].astype(F32)
    for plane in range(2):
        out_ref[plane, 0] = total[plane * rows : (plane + 1) * rows]

    def add_in(received, kind):
        for c in range(CHUNKS):
            piece_copy(received, received, c, kind, across).wait_recv()
            plane, inside = divmod(c * piece, rows)
            out_ref[plane, 0, inside : inside + piece] += received[part(c)].astype(F32)

    @pl.when(odd)
    def _():
        add_in(from_mate, 6)

    @pl.when(tile >= 2)
    def _():
        add_in(from_back, 8)

    @pl.when(tile >= 2)
    def _():
        for c in range(CHUNKS):
            band_copy(core, 0, 2, c, 2, partner).wait_send()

    @pl.when(odd)
    def _():
        for c in range(CHUNKS):
            band_copy(core, 0, 1, c, 1, partner).wait_send()

    @pl.when(tile + 2 < tile_count)
    def _():
        @pl.when(even)
        def _():
            for c in range(CHUNKS):
                band_copy(core, 2, 1, c, 1, partner).wait_send()

        for c in range(CHUNKS):
            band_copy(core, 2, 2, c, 4, partner).wait_send()
        for c in range(CHUNKS):
            piece_copy(to_next, from_back, c, 8, partner).wait_send()

    @pl.when(tile + 1 < tile_count)
    def _():
        for c in range(CHUNKS):
            band_copy(core, 1, 1, c, 3, partner).wait_send()

    for b in range(3):
        swap(b).wait_send()

    @pl.when(even & has_mate)
    def _():
        for c in range(CHUNKS):
            piece_copy(to_mate, from_mate, c, 6, partner).wait_send()

    @pl.when(odd & (tile + 1 < tile_count))
    def _():
        for c in range(CHUNKS):
            piece_copy(to_mate, relayed, c, 7, partner).wait_send()


def shards(
    object_slices, probe_wave, propagator, tile_counts, row_offsets, column_offsets, intensity
):
    size = probe_wave.shape[1]
    rows, width = object_slices.shape[2:]
    mine = row_offsets.shape[0] // lax.axis_size("section")
    tile_count = lax.axis_size("tiles")
    anywhere = pl.BlockSpec(memory_space=pl.ANY)
    vmem = pl.BlockSpec(memory_space=pltpu.VMEM)
    band = pltpu.VMEM((2 * rows, width), BF16)

    def body(*refs):
        kernel(tile_count, *refs)

    return pl.pallas_call(
        body,
        out_shape=jax.ShapeDtypeStruct(object_slices.shape, F32),
        in_specs=[anywhere] * 8,
        out_specs=vmem,
        scratch_shapes=[
            pltpu.SMEM(tile_counts.shape, jnp.int32),
            pltpu.SMEM(row_offsets.shape, jnp.int32),
            pltpu.SMEM(column_offsets.shape, jnp.int32),
            pltpu.VMEM(object_slices.shape, F32),
            pltpu.VMEM(probe_wave.shape, F32),
            pltpu.VMEM(propagator.shape, F32),
            pltpu.VMEM((2, 2 * size, 2 * size), BF16),
            pltpu.VMEM((mine, size, size), F32),
            pltpu.VMEM((2, 3, 2 * rows, width), BF16),
            pltpu.VMEM((2, mine, 3 * rows, 2 * size), BF16),
            pltpu.VMEM((width, mine * size), BF16),
            pltpu.VMEM((mine * size, width), BF16),
            pltpu.VMEM((mine, size, 3 * rows), BF16),
            pltpu.VMEM((mine, 3 * rows, size), BF16),
            pltpu.VMEM((2, 3, 2 * rows, width), F32),
            pltpu.VMEM((3, 2 * rows, width), BF16),
            pltpu.VMEM((3, 2 * rows, width), BF16),
            band,
            band,
            band,
            band,
            band,
            pltpu.SemaphoreType.DMA((9 * CHUNKS,)),
            pltpu.SemaphoreType.DMA((9 * CHUNKS,)),
            pltpu.SemaphoreType.DMA((8,)),
        ],
        compiler_params=pltpu.CompilerParams(
            collective_id=0, has_side_effects=True, vmem_limit_bytes=60 * 1024 * 1024
        ),
    )(
        tile_counts, row_offsets, column_offsets, object_slices, probe_wave, propagator,
        fourier_blocks(size), intensity,
    )


def solution(mesh):
    placed = (
        P(None, "section", ("groups", "tiles"), None),
        P(),
        P(),
        P(("groups", "tiles")),
        P(("groups", "tiles")),
        P(("groups", "tiles")),
        P(("groups", "tiles"), None, None),
    )
    return jax.shard_map(
        shards,
        mesh=mesh,
        in_specs=placed,
        out_specs=P(None, "section", ("groups", "tiles"), None),
        check_vma=False,
    )
```

```python
import math

import jax
import jax.numpy as jnp
import numpy as np
from jax import lax
from jax.experimental import pallas as pl
from jax.experimental.pallas import tpu as pltpu
from jax.sharding import PartitionSpec as P

MESH = pl.DeviceIdType.MESH
BF16 = jnp.bfloat16
CHUNKS = 8
F32 = jnp.float32


def fourier_blocks(wave_size):
    counter = np.arange(wave_size)
    turned = (counter[:, None] * counter[None, :] % wave_size).astype(np.float32)
    angles = turned * np.float32(2.0 * math.pi / wave_size)
    factor = np.float32(1.0 / math.sqrt(wave_size))
    real = (np.cos(angles) * factor).astype(np.float32)
    imag = (-np.sin(angles) * factor).astype(np.float32)
    plain = np.block([[real, imag], [-imag, real]])
    turned = np.block([[real, -imag], [imag, real]])
    return jnp.asarray(np.stack([plain, turned]).astype(jnp.bfloat16))


def dot(left_side, right_side):
    return jnp.dot(left_side, right_side, preferred_element_type=F32)


def sandwich(left_block, right_block, waves):
    size = waves[0][0].shape[0]
    stacked = jnp.concatenate([jnp.concatenate([real, imag], axis=0) for real, imag in waves], axis=1)
    halfway = dot(left_block, stacked).astype(BF16)
    results = []
    for p in range(len(waves)):
        columns = slice(p * size, (p + 1) * size)
        row = jnp.concatenate([halfway[:size, columns], halfway[size:, columns]], axis=1)
        full = dot(row, right_block)
        results.append((full[:, :size], full[:, size:]))
    return results


def times(a, b):
    return (a[0] * b[0] - a[1] * b[1], a[0] * b[1] + a[1] * b[0])


def conj_times(a, b):
    return (a[0] * b[0] + a[1] * b[1], a[0] * b[1] - a[1] * b[0])


def cast(pair, dtype):
    return (pair[0].astype(dtype), pair[1].astype(dtype))


def kernel(
    tile_count, counts_hbm, row_offsets_hbm, column_offsets_hbm, object_hbm, probe_hbm, propagator_hbm,
    fourier_hbm, intensity_hbm, out_ref, counts, row_offsets, column_offsets, object_ref, probe_ref,
    propagator_ref, fourier_ref, measured, bands, strips, pick, place, pick_rows, place_rows, partial,
    to_partner, from_partner, to_next, to_mate, from_back, from_mate, relayed, send_sem, recv_sem, load_sem,
):
    size = probe_ref.shape[1]
    rows = object_ref.shape[2]
    width = object_ref.shape[3]
    mine = measured.shape[0]
    tile = lax.axis_index("tiles")
    core = lax.axis_index("section")
    other = 1 - core
    first = core * mine
    odd = lax.rem(tile, 2) == 1
    even = lax.rem(tile, 2) == 0
    mate = tile + 1 - 2 * lax.rem(tile, 2)
    has_mate = mate < tile_count

    loads = [
        pltpu.make_async_copy(source, held, load_sem.at[i])
        for i, (source, held) in enumerate(
            [
                (object_hbm, object_ref),
                (row_offsets_hbm, row_offsets),
                (column_offsets_hbm, column_offsets),
                (counts_hbm, counts),
                (propagator_hbm, propagator_ref),
                (fourier_hbm, fourier_ref),
                (probe_hbm, probe_ref),
                (intensity_hbm.at[pl.ds(first, mine)], measured),
            ]
        )
    ]
    for load in loads:
        load.start()

    def remote(src, dst, index, where):
        return pltpu.make_async_remote_copy(
            src_ref=src, dst_ref=dst, send_sem=send_sem.at[index], recv_sem=recv_sem.at[index],
            device_id=where, device_id_type=MESH,
        )

    partner = {"section": other}
    to_back = {"tiles": tile - 2}
    to_ahead = {"tiles": tile + 2}
    across = {"tiles": mate}

    barrier = pltpu.get_barrier_semaphore()
    pl.semaphore_signal(barrier, inc=1, device_id=partner, device_id_type=MESH)
    arrivals = jnp.int32(1)
    for there, where in ((tile >= 2, to_back), (tile + 2 < tile_count, to_ahead), (has_mate, across)):
        arrivals = arrivals + there.astype(jnp.int32)

        @pl.when(there)
        def _():
            pl.semaphore_signal(barrier, inc=1, device_id=where, device_id_type=MESH)

    loads[0].wait()
    for plane in range(2):
        bands[core, 0, plane * rows : (plane + 1) * rows, :] = object_ref[plane, 0].astype(BF16)
    pl.semaphore_wait(barrier, arrivals)

    piece = 2 * rows // CHUNKS

    def part(c):
        return pl.ds(c * piece, piece)

    def chunk(layer, b, c):
        return bands.at[layer, b, part(c)]

    def band_copy(layer, source, target, c, kind, where):
        return remote(chunk(layer, source, c), chunk(layer, target, c), CHUNKS * kind + c, where)

    @pl.when(tile >= 2)
    def _():
        for c in range(CHUNKS):
            band_copy(core, 0, 2, c, 2, to_back).start()

    @pl.when(odd)
    def _():
        for c in range(CHUNKS):
            band_copy(core, 0, 1, c, 1, across).start()

    for c in range(CHUNKS):
        band_copy(core, 0, 0, c, 0, partner).start()

    for load in loads[1:7]:
        load.wait()

    spots = lax.broadcasted_iota(jnp.int32, (size, width), 1)
    counter = lax.broadcasted_iota(jnp.int32, (size, width), 0)
    down_spots = lax.broadcasted_iota(jnp.int32, (width, size), 0)
    down_counter = lax.broadcasted_iota(jnp.int32, (width, size), 1)
    row_spots = lax.broadcasted_iota(jnp.int32, (size, 3 * rows), 1)
    row_counter = lax.broadcasted_iota(jnp.int32, (size, 3 * rows), 0)
    down_row_spots = lax.broadcasted_iota(jnp.int32, (3 * rows, size), 0)
    down_row_counter = lax.broadcasted_iota(jnp.int32, (3 * rows, size), 1)
    for p in range(mine):
        column = column_offsets[first + p]
        offset = row_offsets[first + p]
        pick[:, p * size : (p + 1) * size] = jnp.where(down_spots == down_counter + column, 1.0, 0.0).astype(BF16)
        place[p * size : (p + 1) * size, :] = jnp.where(spots == counter + column, 1.0, 0.0).astype(BF16)
        pick_rows[p] = jnp.where(row_spots == row_counter + offset, 1.0, 0.0).astype(BF16)
        place_rows[p] = jnp.where(down_row_spots == down_row_counter + offset, 1.0, 0.0).astype(BF16)
    prop = (propagator_ref[0].astype(BF16), propagator_ref[1].astype(BF16))

    def block(a, b, c, d):
        return jnp.concatenate([jnp.concatenate([a, b], axis=1), jnp.concatenate([c, d], axis=1)], axis=0)

    prop_plain = block(prop[0], prop[1], -prop[1], prop[0])
    prop_turned = block(prop[0], -prop[1], prop[1], prop[0])
    four_plain = fourier_ref[0]
    four_turned = fourier_ref[1]

    def extract(layer, b):
        found = dot(bands[layer, b], pick[...]).astype(BF16)
        for p in range(mine):
            for plane in range(2):
                strips[layer, p, b * rows : (b + 1) * rows, plane * size : (plane + 1) * size] = found[
                    plane * rows : (plane + 1) * rows, p * size : (p + 1) * size
                ]

    for ahead in (1, 2):

        @pl.when(tile + ahead >= tile_count)
        def _():
            for layer in range(2):
                bands[layer, ahead] = jnp.zeros((2 * rows, width), BF16)

    extract(core, 0)
    for c in range(CHUNKS):
        band_copy(core, 0, 0, c, 0, partner).wait()
    extract(other, 0)

    @pl.when(tile + 2 < tile_count)
    def _():
        for c in range(CHUNKS):
            band_copy(core, 2, 2, c, 2, partner).wait_recv()

            @pl.when(even)
            def _():
                band_copy(core, 2, 1, c, 1, across).start()

            band_copy(core, 2, 2, c, 4, partner).start()

    extract(core, 2)

    @pl.when(tile + 1 < tile_count)
    def _():
        for c in range(CHUNKS):
            band_copy(core, 1, 1, c, 1, partner).wait_recv()
            band_copy(core, 1, 1, c, 3, partner).start()

    extract(core, 1)

    @pl.when(tile + 2 < tile_count)
    def _():
        for c in range(CHUNKS):
            band_copy(other, 2, 2, c, 4, partner).wait_recv()

    extract(other, 2)

    @pl.when(tile + 1 < tile_count)
    def _():
        for c in range(CHUNKS):
            band_copy(other, 1, 1, c, 3, partner).wait_recv()

    extract(other, 1)

    patches = [[None] * mine for _ in range(2)]
    for layer in range(2):
        for p in range(mine):
            found = dot(pick_rows[p], strips[layer, p])
            patches[layer][p] = (found[:, :size], found[:, size:])

    start = (probe_ref[0].astype(BF16).astype(F32), probe_ref[1].astype(BF16).astype(F32))
    product = [cast(times(start, patches[0][p]), BF16) for p in range(mine)]
    middle = [cast(z, BF16) for z in sandwich(prop_turned, prop_plain, product)]
    product = [cast(times(cast(middle[p], F32), patches[1][p]), BF16) for p in range(mine)]
    exit_waves = [cast(z, BF16) for z in sandwich(prop_turned, prop_plain, product)]
    far = sandwich(four_turned, four_plain, exit_waves)
    loads[7].wait()
    misfit = []
    for p in range(mine):
        real, imag = far[p]
        excess = real * real + imag * imag - measured[p]
        live = jnp.full((size, size), first + p, jnp.int32) < counts[0]
        misfit.append(
            (jnp.where(live, excess * real, 0.0).astype(BF16), jnp.where(live, excess * imag, 0.0).astype(BF16))
        )
    adjoint = [cast(z, BF16) for z in sandwich(four_plain, four_turned, misfit)]

    def deposit(layer, gradients):
        shifted = [
            dot(place_rows[p], jnp.concatenate(cast(gradients[p], BF16), axis=1)).astype(BF16) for p in range(mine)
        ]
        for b in (1, 2, 0):
            pieces = [
                jnp.concatenate(
                    [s[b * rows : (b + 1) * rows, plane * size : (plane + 1) * size] for s in shifted], axis=1
                )
                for plane in range(2)
            ]
            partial[layer, b] = dot(jnp.concatenate(pieces, axis=0), place[...])

    def swap(b):
        return remote(to_partner.at[b], from_partner.at[b], 5 * CHUNKS + b, partner)

    def piece_copy(source, target, c, kind, where):
        return remote(source.at[part(c)], target.at[part(c)], CHUNKS * kind + c, where)

    def give(layer):
        @pl.when(core != layer)
        def _():
            for b in (1, 2, 0):
                to_partner[b] = partial[layer, b].astype(BF16)
                swap(b).start()

    def hand_over(layer):
        @pl.when(core == layer)
        def _():
            swap(1).wait_recv()
            for c in range(CHUNKS):
                to_mate[part(c)] = (partial[layer, 1, part(c)] + from_partner[1, part(c)].astype(F32)).astype(BF16)

                @pl.when(even & has_mate)
                def _():
                    piece_copy(to_mate, from_mate, c, 6, across).start()

                @pl.when(odd & (tile + 1 < tile_count))
                def _():
                    piece_copy(to_mate, relayed, c, 7, across).start()

            swap(2).wait_recv()

            @pl.when(odd & (tile + 2 < tile_count))
            def _():
                for c in range(CHUNKS):
                    total = partial[layer, 2, part(c)] + from_partner[2, part(c)].astype(F32)
                    to_next[part(c)] = total.astype(BF16)
                    piece_copy(to_next, from_back, c, 8, to_ahead).start()

    def send_relayed(layer):
        @pl.when((core == layer) & even & (tile + 2 < tile_count))
        def _():
            for c in range(CHUNKS):
                total = partial[layer, 2, part(c)] + from_partner[2, part(c)].astype(F32)
                piece_copy(to_mate, relayed, c, 7, across).wait_recv()
                to_next[part(c)] = (total + relayed[part(c)].astype(F32)).astype(BF16)
                piece_copy(to_next, from_back, c, 8, to_ahead).start()

    back = sandwich(prop_plain, prop_turned, adjoint)
    deposit(1, [conj_times(cast(middle[p], F32), back[p]) for p in range(mine)])
    give(1)
    adjoint = [cast(conj_times(patches[1][p], back[p]), BF16) for p in range(mine)]
    back = sandwich(prop_plain, prop_turned, adjoint)
    gradients = [conj_times(start, back[p]) for p in range(mine)]
    hand_over(1)
    deposit(0, gradients)
    give(0)
    send_relayed(1)
    hand_over(0)
    send_relayed(0)

    swap(0).wait_recv()
    total = partial[core, 0] + from_partner[0].astype(F32)
    for plane in range(2):
        out_ref[plane, 0] = total[plane * rows : (plane + 1) * rows]

    def add_in(received, kind):
        for c in range(CHUNKS):
            piece_copy(received, received, c, kind, across).wait_recv()
            plane, inside = divmod(c * piece, rows)
            out_ref[plane, 0, inside : inside + piece] += received[part(c)].astype(F32)

    @pl.when(odd)
    def _():
        add_in(from_mate, 6)

    @pl.when(tile >= 2)
    def _():
        add_in(from_back, 8)

    @pl.when(tile >= 2)
    def _():
        for c in range(CHUNKS):
            band_copy(core, 0, 2, c, 2, partner).wait_send()

    @pl.when(odd)
    def _():
        for c in range(CHUNKS):
            band_copy(core, 0, 1, c, 1, partner).wait_send()

    @pl.when(tile + 2 < tile_count)
    def _():
        @pl.when(even)
        def _():
            for c in range(CHUNKS):
                band_copy(core, 2, 1, c, 1, partner).wait_send()

        for c in range(CHUNKS):
            band_copy(core, 2, 2, c, 4, partner).wait_send()
        for c in range(CHUNKS):
            piece_copy(to_next, from_back, c, 8, partner).wait_send()

    @pl.when(tile + 1 < tile_count)
    def _():
        for c in range(CHUNKS):
            band_copy(core, 1, 1, c, 3, partner).wait_send()

    for b in range(3):
        swap(b).wait_send()

    @pl.when(even & has_mate)
    def _():
        for c in range(CHUNKS):
            piece_copy(to_mate, from_mate, c, 6, partner).wait_send()

    @pl.when(odd & (tile + 1 < tile_count))
    def _():
        for c in range(CHUNKS):
            piece_copy(to_mate, relayed, c, 7, partner).wait_send()


def shards(
    object_slices, probe_wave, propagator, tile_counts, row_offsets, column_offsets, intensity
):
    size = probe_wave.shape[1]
    rows, width = object_slices.shape[2:]
    mine = row_offsets.shape[0] // lax.axis_size("section")
    tile_count = lax.axis_size("tiles")
    anywhere = pl.BlockSpec(memory_space=pl.ANY)
    vmem = pl.BlockSpec(memory_space=pltpu.VMEM)
    band = pltpu.VMEM((2 * rows, width), BF16)

    def body(*refs):
        kernel(tile_count, *refs)

    return pl.pallas_call(
        body,
        out_shape=jax.ShapeDtypeStruct(object_slices.shape, F32),
        in_specs=[anywhere] * 8,
        out_specs=vmem,
        scratch_shapes=[
            pltpu.SMEM(tile_counts.shape, jnp.int32),
            pltpu.SMEM(row_offsets.shape, jnp.int32),
            pltpu.SMEM(column_offsets.shape, jnp.int32),
            pltpu.VMEM(object_slices.shape, F32),
            pltpu.VMEM(probe_wave.shape, F32),
            pltpu.VMEM(propagator.shape, F32),
            pltpu.VMEM((2, 2 * size, 2 * size), BF16),
            pltpu.VMEM((mine, size, size), F32),
            pltpu.VMEM((2, 3, 2 * rows, width), BF16),
            pltpu.VMEM((2, mine, 3 * rows, 2 * size), BF16),
            pltpu.VMEM((width, mine * size), BF16),
            pltpu.VMEM((mine * size, width), BF16),
            pltpu.VMEM((mine, size, 3 * rows), BF16),
            pltpu.VMEM((mine, 3 * rows, size), BF16),
            pltpu.VMEM((2, 3, 2 * rows, width), F32),
            pltpu.VMEM((3, 2 * rows, width), BF16),
            pltpu.VMEM((3, 2 * rows, width), BF16),
            band,
            band,
            band,
            band,
            band,
            pltpu.SemaphoreType.DMA((9 * CHUNKS,)),
            pltpu.SemaphoreType.DMA((9 * CHUNKS,)),
            pltpu.SemaphoreType.DMA((8,)),
        ],
        compiler_params=pltpu.CompilerParams(
            collective_id=0, has_side_effects=True, vmem_limit_bytes=60 * 1024 * 1024
        ),
    )(
        tile_counts, row_offsets, column_offsets, object_slices, probe_wave, propagator,
        fourier_blocks(size), intensity,
    )


def solution(mesh):
    placed = (
        P(None, "section", ("groups", "tiles"), None),
        P(),
        P(),
        P(("groups", "tiles")),
        P(("groups", "tiles")),
        P(("groups", "tiles")),
        P(("groups", "tiles"), None, None),
    )
    return jax.shard_map(
        shards,
        mesh=mesh,
        in_specs=placed,
        out_specs=P(None, "section", ("groups", "tiles"), None),
        check_vma=False,
    )
```
